32 devices in a mesh: tmpl: 4 (over y, x), row: 2 (over core), col: 4 (over z).
Axes of the slice: x: 2, y: 2, z: 4, core: 2. Of those that a mesh axis runs over, the one named last changes fastest.
Arguments:
- tmpl_act: bfloat16 [4, 4, 512, 64, 2048], P('tmpl', None, 'row', None, 'col'), may hold values from -4 to 4
- tmpl_bins: int32 [4, 4, 512, 2048], P('tmpl', None, 'row', 'col'), may hold values from 0 to 38
- tmpl_mask: int32 [4, 2048], P('tmpl'), may hold values 0 or 1
- tmpl_aatype: int32 [4, 2048], P('tmpl'), may hold values from 0 to 21
- pair_act: bfloat16 [2048, 2048, 128], P(('tmpl', 'row', 'col')), may hold values from -2.5 to 2.5
- labels: int32 [2048, 2048], P(('tmpl', 'row', 'col')), may hold values from 0 to 63
- bin_embed: bfloat16 [39, 64], replicated, may hold values from -4 to 4
- row_embed: bfloat16 [22, 64], replicated, may hold values from -4 to 4
- col_embed: bfloat16 [22, 64], replicated, may hold values from -4 to 4
- mask_embed: float32 [64], replicated, may hold values from -4 to 4
- layer_gain: float32 [2, 64], replicated, may hold values from 0.1 to 1.9
- w_in: bfloat16 [2, 64, 128], replicated, may hold values from -0.75 to 0.75
- w_out: bfloat16 [2, 128, 64], replicated, may hold values from -0.5 to 0.5
- final_gain: float32 [64], replicated, may hold values from 0.1 to 1.9
- w_query: bfloat16 [128, 64], replicated, may hold values from -0.5 to 0.5
- w_keyval: bfloat16 [64, 128], replicated, may hold values from -0.75 to 0.75
- w_output: bfloat16 [64, 128], replicated, may hold values from -0.75 to 0.75
- head_weight: bfloat16 [128, 64], replicated, may hold values from -0.44921875 to 0.44921875
- head_bias: float32 [64], replicated, may hold values from -3 to 3
Outputs:
- mean_loss: float32 [], replicated
- head_grad: float32 [128, 64], replicated
- bias_grad: float32 [64], replicated
- output_grad: float32 [64, 128], replicated
The draws below stay inside these ranges and needn't reach their ends.
All inputs are finite; a program needn't handle non-finite values. No bound on the sum of `tmpl_mask` on one device may be relied on, other than what follows from the above.
Results may differ from the reference program's by a relative error of at most 0.0003.
Values may be sent and summed in bfloat16 or wider, within the bound.
A program may use at most 512 MiB of HBM per device.

```python
import math
import jax
import jax.numpy as jnp
from jax import lax

S = 4
C = 64
CZ = 128
HEADS = 4
HEAD_DIM = 16
HIDDEN_SIZE = 128
NBIN = 39
NAA = 22
NB = 64
TLAYERS = 2
N = 2048
GROUPS = 4
HD = 64


def with_ends(array, stream_key, least, largest):
    longest = array.shape.index(max(array.shape))
    spots = []
    for shift in (0, 1):
        where = [jax.random.randint(jax.random.fold_in(stream_key, axis), (), 0, length) for axis, length in enumerate(array.shape)]
        where[longest] = (where[longest] + shift) % array.shape[longest]
        spots.append(tuple(where))
    return array.at[spots[0]].set(least).at[spots[1]].set(largest)


def steps_of(key, dims, cuts, least, high):
    factor_of = 1.0
    for dim, blocks in cuts:
        draws = jax.random.uniform(jax.random.fold_in(jax.random.fold_in(key, 6), dim), (blocks,), jnp.float32, least / len(cuts), high / len(cuts))
        factor_of = factor_of * jnp.repeat(jnp.exp(draws), dims[dim] // blocks).reshape((-1,) + (1,) * (len(dims) - 1 - dim))
    return factor_of


def normal_values(own_key, extent, width, limit, cuts=(), kind=jnp.bfloat16):
    loudness = steps_of(own_key, extent, cuts, -0.22, 0.18) if cuts else 1.0
    drawn = jax.random.normal(own_key, extent, jnp.float32) * width * loudness
    return jnp.minimum(jnp.maximum(drawn, -limit), limit).astype(kind)


def setup_inputs(seed: int = 0) -> dict:
    streams_of = jax.random.split(jax.random.key(seed), 20)
    tmpl_act = normal_values(streams_of[0], (S, GROUPS, N // GROUPS, C, N), 1.0, 4.0, ((0, 4), (2, 2), (4, 4)))
    tmpl_bins = with_ends(jax.random.randint(streams_of[1], (S, GROUPS, N // GROUPS, N), 0, NBIN), jax.random.fold_in(streams_of[1], 1), 0, NBIN - 1).astype(jnp.int32)
    tmpl_mask = with_ends((jax.random.randint(streams_of[2], (S, N), 0, 5) < 4).astype(jnp.int32), jax.random.fold_in(streams_of[2], 1), 0, 1)
    tmpl_aatype = with_ends(jax.random.randint(streams_of[3], (S, N), 0, NAA), jax.random.fold_in(streams_of[3], 1), 0, NAA - 1).astype(jnp.int32)
    pair_act = normal_values(streams_of[4], (N, N, CZ), 1.0, 2.5, ((0, 32),))
    labels = with_ends(jax.random.randint(streams_of[5], (N, N), 0, NB), jax.random.fold_in(streams_of[5], 1), 0, NB - 1).astype(jnp.int32)
    bin_embed = normal_values(streams_of[6], (NBIN, C), 1.0, 4.0)
    row_embed = normal_values(streams_of[7], (NAA, C), 1.0, 4.0)
    col_embed = normal_values(streams_of[8], (NAA, C), 1.0, 4.0)
    mask_embed = normal_values(streams_of[9], (C,), 1.0, 4.0, (), jnp.float32)
    layer_gain = jnp.clip(1.0 + 0.18 * jax.random.normal(streams_of[10], (TLAYERS, C), jnp.float32), 0.1, 1.9)
    w_in = normal_values(streams_of[11], (TLAYERS, C, HIDDEN_SIZE), C ** -0.5, 0.75)
    w_out = normal_values(streams_of[12], (TLAYERS, HIDDEN_SIZE, C), HIDDEN_SIZE ** -0.5, 0.5)
    final_gain = jnp.clip(1.0 + 0.18 * jax.random.normal(streams_of[13], (C,), jnp.float32), 0.1, 1.9)
    w_query = normal_values(streams_of[14], (CZ, HD), CZ ** -0.5, 0.5)
    w_keyval = normal_values(streams_of[15], (C, 2 * HD), C ** -0.5, 0.75)
    w_output = normal_values(streams_of[16], (HD, CZ), HD ** -0.5, 0.75)
    head_weight = jnp.clip(jax.random.uniform(streams_of[17], (CZ, NB), jnp.float32, -0.44921875, 0.44921875), -0.44921875, 0.44921875).astype(jnp.bfloat16)
    head_bias = normal_values(streams_of[18], (NB,), 1.0, 3.0, (), jnp.float32)
    return {"tmpl_act": tmpl_act, "tmpl_bins": tmpl_bins, "tmpl_mask": tmpl_mask, "tmpl_aatype": tmpl_aatype, "pair_act": pair_act, "labels": labels, "bin_embed": bin_embed, "row_embed": row_embed, "col_embed": col_embed, "mask_embed": mask_embed, "layer_gain": layer_gain, "w_in": w_in, "w_out": w_out, "final_gain": final_gain, "w_query": w_query, "w_keyval": w_keyval, "w_output": w_output, "head_weight": head_weight, "head_bias": head_bias}


CLIP_NORM = 16.0

def layer_norm(inputs, gain_vector, channel_axis):
    average = lax.optimization_barrier(jnp.mean(inputs, axis=channel_axis, keepdims=True))
    centered = inputs - average
    spread = lax.optimization_barrier(jnp.mean(centered * centered, axis=channel_axis, keepdims=True))
    return centered * lax.rsqrt(spread + 1e-05) * gain_vector

def reference(tmpl_act, tmpl_bins, tmpl_mask, tmpl_aatype, pair_act, labels, bin_embed, row_embed, col_embed, mask_embed, layer_gain, w_in, w_out, final_gain, w_query, w_keyval, w_output, head_weight, head_bias):
    row_block = 64
    head_width = HEADS * HEAD_DIM
    activations = tmpl_act.reshape(S, N, C, N)
    bin_codes = tmpl_bins.reshape(S, N, N)
    mask_table = tmpl_mask.astype(jnp.float32)
    bin_table = bin_embed.astype(jnp.float32)
    row_table = row_embed.astype(jnp.float32)
    col_terms = col_embed.astype(jnp.float32)[tmpl_aatype]
    levels = jnp.arange(NBIN, dtype=jnp.int32)
    classes = jnp.arange(NB, dtype=jnp.int32)
    w_query32 = w_query.astype(jnp.float32)
    w_keyval32 = w_keyval.astype(jnp.float32)
    w_output32 = w_output.astype(jnp.float32)
    head32 = head_weight.astype(jnp.float32)

    def one_block(offset):
        features = []
        for template in range(S):
            previous = lax.dynamic_slice_in_dim(activations[template], offset, row_block, 0).astype(jnp.float32)
            previous = jnp.swapaxes(previous, 1, 2)
            codes = lax.dynamic_slice_in_dim(bin_codes[template], offset, row_block, 0)
            onehot = (codes[:, :, None] == levels).astype(jnp.float32)
            bin_term = jnp.einsum('ijb,bc->ijc', onehot, bin_table)
            row_mask = lax.dynamic_slice_in_dim(mask_table[template], offset, row_block, 0)
            row_types = lax.dynamic_slice_in_dim(tmpl_aatype[template], offset, row_block, 0)
            pair_mask = row_mask[:, None] * mask_table[template][None, :]
            tmpl_state = previous + pair_mask[:, :, None] * (bin_term + mask_embed) + row_table[row_types][:, None, :] + col_terms[template][None, :, :]
            for layer_index in range(TLAYERS):
                normed = layer_norm(tmpl_state, layer_gain[layer_index], -1).astype(jnp.bfloat16)
                hidden = jax.nn.relu(jnp.einsum('ijc,ce->ije', normed.astype(jnp.float32), w_in[layer_index].astype(jnp.float32))).astype(jnp.bfloat16)
                tmpl_state = tmpl_state + jnp.einsum('ije,ec->ijc', hidden.astype(jnp.float32), w_out[layer_index].astype(jnp.float32))
            features.append(layer_norm(tmpl_state, final_gain, -1).astype(jnp.bfloat16))
        features = jnp.stack(features).astype(jnp.float32)
        pair_rows = lax.dynamic_slice_in_dim(pair_act, offset, row_block, 0).astype(jnp.float32)
        queries = jnp.einsum('ijz,zk->ijk', pair_rows, w_query32).astype(jnp.bfloat16).astype(jnp.float32)
        queries = queries.reshape(row_block, N, HEADS, HEAD_DIM)
        keyval = jnp.einsum('sijc,ck->sijk', features, w_keyval32).astype(jnp.bfloat16).astype(jnp.float32)
        key_heads = keyval[..., :head_width].reshape(S, row_block, N, HEADS, HEAD_DIM)
        value_heads = keyval[..., head_width:].reshape(S, row_block, N, HEADS, HEAD_DIM)
        scores = jnp.einsum('ijhd,sijhd->sijh', queries, key_heads) / math.sqrt(HEAD_DIM)
        exp_scores = jnp.exp(scores)
        weights = (exp_scores / lax.optimization_barrier(jnp.sum(exp_scores, axis=0, keepdims=True))).astype(jnp.bfloat16).astype(jnp.float32)
        mixture = jnp.einsum('sijh,sijhd->ijhd', weights, value_heads).astype(jnp.bfloat16).astype(jnp.float32)
        mixture = mixture.reshape(row_block, N, head_width)
        new_pair = (pair_rows + jnp.einsum('ijk,kz->ijz', mixture, w_output32)).astype(jnp.bfloat16).astype(jnp.float32)
        logits = jnp.einsum('ijz,zb->ijb', new_pair, head32) + head_bias
        exp_logits = jnp.exp(logits)
        partition = lax.optimization_barrier(jnp.sum(exp_logits, axis=-1, keepdims=True))
        label_rows = lax.dynamic_slice_in_dim(labels, offset, row_block, 0)
        target = (label_rows[:, :, None] == classes).astype(jnp.float32)
        cross_entropy = jnp.log(partition[..., 0]) - lax.optimization_barrier(jnp.sum(target * logits, axis=-1))
        logit_grad = ((exp_logits / partition - target) / N).astype(jnp.bfloat16).astype(jnp.float32)
        head_part = jnp.einsum('ijz,ijb->zb', new_pair, logit_grad)
        bias_part = lax.optimization_barrier(jnp.sum(logit_grad, axis=(0, 1)))
        pair_grad = jnp.einsum('ijb,zb->ijz', logit_grad, head32).astype(jnp.bfloat16).astype(jnp.float32)
        output_part = jnp.einsum('ijk,ijz->kz', mixture, pair_grad)
        return (jnp.sum(cross_entropy), head_part, bias_part, output_part)
    offsets = jnp.arange(N // row_block, dtype=jnp.int32) * row_block
    losses, head_parts, bias_parts, output_parts = lax.map(one_block, offsets)
    loss_sum = jnp.sum(losses)
    head_sum = lax.optimization_barrier(jnp.sum(head_parts, axis=0))
    bias_sum = lax.optimization_barrier(jnp.sum(bias_parts, axis=0))
    output_sum = lax.optimization_barrier(jnp.sum(output_parts, axis=0))
    squares = jnp.sum(head_sum * head_sum) + jnp.sum(bias_sum * bias_sum) + jnp.sum(output_sum * output_sum)
    factor = CLIP_NORM / jnp.maximum(jnp.sqrt(squares), CLIP_NORM)
    return (loss_sum / float(N * N), head_sum * factor, bias_sum * factor, output_sum * factor)
```

```python
import functools
import math

import jax
import jax.numpy as jnp
from jax import lax
from jax.experimental import pallas as pl
from jax.experimental.pallas import tpu as pltpu
from jax.sharding import PartitionSpec as P

HEADS = 4
HEAD_DIM = 16
CLIP_NORM = 16.0
TILE = 16
BF16 = jnp.bfloat16
F32 = jnp.float32


def padded(size):
    return -(-size // TILE) * TILE


def pad_columns(matrix):
    return jnp.pad(matrix, ((0, 0), (0, padded(matrix.shape[1]) - matrix.shape[1])))


def layer_norm(state, gain):
    count = state.shape[0]
    average = jnp.sum(state, axis=0, keepdims=True) * (1.0 / count)
    centered = state - average
    spread = jnp.sum(centered * centered, axis=0, keepdims=True) * (1.0 / count)
    return (centered * lax.rsqrt(spread + 1e-05) * gain).astype(BF16)


def dot(left, right):
    return lax.dot_general(left, right, (((1,), (0,)), ((), ())), preferred_element_type=F32)


def dot_lanes(left, right):
    return lax.dot_general(left, right, (((1,), (1,)), ((), ())), preferred_element_type=F32)


def template_kernel(
    levels,
    together,
    place_ref,
    mask_ref,
    type_ref,
    act_ref,
    bins_ref,
    colmask_ref,
    colhot_ref,
    embed_ref,
    gains_ref,
    w_in_ref,
    w_out_ref,
    out_ref,
):
    rows = act_ref.shape[1]
    width = act_ref.shape[3]
    offset = place_ref[2] + pl.program_id(0) * rows
    level_rows = padded(levels + 3)
    kind_rows = colhot_ref.shape[0]
    layers = w_in_ref.shape[0]

    def some_rows(step, carry):
        level_iota = lax.broadcasted_iota(jnp.int32, (level_rows, width), 0)
        least = jnp.where(
            level_iota < levels, level_iota, jnp.where(level_iota < levels + 3, 0, levels)
        )
        most = jnp.where(
            level_iota < levels, level_iota, jnp.where(level_iota < levels + 3, levels - 1, -1)
        )
        kind_iota = lax.broadcasted_iota(jnp.int32, (kind_rows, width), 0)
        states = []
        for inner in range(together):
            row = step * together + inner
            row_mask = mask_ref[offset + row]
            row_type = type_ref[offset + row]
            codes = bins_ref[0, pl.ds(row, 1), :]
            codes = jnp.where(colmask_ref[...] * row_mask > 0, codes, -1)
            hot = jnp.where((codes >= least) & (codes <= most), 1.0, 0.0).astype(BF16)
            row_hot = jnp.where(kind_iota == row_type, 1.0, 0.0).astype(BF16)
            parts = jnp.concatenate([act_ref[0, row], hot, colhot_ref[...], row_hot], axis=0)
            states.append(dot(embed_ref[...], parts))
        for layer in range(layers):
            normed = [layer_norm(state, gains_ref[layer]) for state in states]
            hidden = [jnp.maximum(dot(w_in_ref[layer], one).astype(BF16), 0) for one in normed]
            states = [state + dot(w_out_ref[layer], one) for state, one in zip(states, hidden)]
        for inner in range(together):
            out_ref[step * together + inner] = layer_norm(states[inner], gains_ref[layers])
        return carry

    lax.fori_loop(0, rows // together, some_rows, 0)


def template_features(
    act, bins, place, masks, types, colmask, colhot, embed, gains, w_in, w_out, levels, row_count
):
    channels, width = act.shape[2:]
    block = math.gcd(8, row_count)
    together = math.gcd(4, block)
    whole = lambda array: pl.BlockSpec(array.shape, lambda r, *_: (0,) * array.ndim)
    pairs = row_count * width
    grid_spec = pltpu.PrefetchScalarGridSpec(
        num_scalar_prefetch=3,
        grid=(row_count // block,),
        in_specs=[
            pl.BlockSpec(
                (1, block, channels, width),
                lambda r, place, *_: (place[0], place[1] * (row_count // block) + r, 0, 0),
            ),
            pl.BlockSpec(
                (1, block, width),
                lambda r, place, *_: (place[0], place[1] * (row_count // block) + r, 0),
            ),
            whole(colmask),
            whole(colhot),
            whole(embed),
            whole(gains),
            whole(w_in),
            whole(w_out),
        ],
        out_specs=pl.BlockSpec((block, channels, width), lambda r, *_: (r, 0, 0)),
    )
    return pl.pallas_call(
        functools.partial(template_kernel, levels, together),
        grid_spec=grid_spec,
        out_shape=jax.ShapeDtypeStruct((row_count, channels, width), BF16),
        compiler_params=pltpu.CompilerParams(vmem_limit_bytes=48 * 2**20),
        cost_estimate=pl.CostEstimate(
            flops=pairs * 2 * 256 * 448, bytes_accessed=pairs * channels * 4, transcendentals=0
        ),
        name="template_features",
    )(place, masks, types, act, bins, colmask, colhot, embed, gains, w_in, w_out)


def pair_kernel(
    together,
    residues,
    *refs,
):
    feature_refs = refs[:-11]
    (
        pair_ref,
        labels_ref,
        w_first_ref,
        w_keyval_ref,
        w_output_ref,
        head_t_ref,
        head_ref,
        bias_ref,
        loss_ref,
        head_part_ref,
        output_part_ref,
    ) = refs[-11:]
    rows, width, pair_width = pair_ref.shape
    bins = head_ref.shape[1]
    head_width = HEADS * HEAD_DIM

    @pl.when(pl.program_id(0) == 0)
    def _():
        loss_ref[...] = jnp.zeros_like(loss_ref)
        head_part_ref[...] = jnp.zeros_like(head_part_ref)
        output_part_ref[...] = jnp.zeros_like(output_part_ref)

    def some_rows(step, carry):
        class_iota = lax.broadcasted_iota(jnp.int32, (bins, width), 0)
        ones = jnp.ones((TILE, width), BF16)
        kept = []
        for inner in range(together):
            row = step * together + inner
            first = dot_lanes(w_first_ref[...], pair_ref[row])
            queries = first[:head_width].astype(BF16).astype(F32)
            scores, values = [], []
            for feature_ref in feature_refs:
                keyval = dot(w_keyval_ref[...], feature_ref[row]).astype(BF16).astype(F32)
                product = (queries * keyval[:head_width]).reshape(HEADS, HEAD_DIM, width)
                scores.append(
                    jnp.exp(jnp.sum(product, axis=1, keepdims=True) * (1.0 / math.sqrt(HEAD_DIM)))
                )
                values.append(keyval[head_width:].reshape(HEADS, HEAD_DIM, width))
            inverse = 1.0 / functools.reduce(jnp.add, scores)
            mixture = functools.reduce(
                jnp.add,
                [
                    (score * inverse).astype(BF16).astype(F32) * value
                    for score, value in zip(scores, values)
                ],
            )
            mixture = mixture.reshape(head_width, width).astype(BF16)
            kept.append((row, first[head_width:], mixture))
        for row, pair, mixture in kept:
            new_pair = (pair + dot(w_output_ref[...], mixture)).astype(BF16)
            logits = dot(head_t_ref[...], new_pair) + bias_ref[...]
            exp_logits = jnp.exp(logits)
            partition = jnp.sum(exp_logits, axis=0, keepdims=True)
            target = class_iota == labels_ref[pl.ds(row, 1), :]
            picked = jnp.sum(jnp.where(target, logits, 0.0), axis=0, keepdims=True)
            loss_ref[...] += jnp.log(partition) - picked
            softmax = exp_logits * (1.0 / partition)
            grad = (jnp.where(target, softmax - 1.0, softmax) * (1.0 / residues)).astype(BF16)
            head_part_ref[...] += dot_lanes(grad, jnp.concatenate([new_pair, ones], axis=0))
            pair_grad = dot(head_ref[...], grad).astype(BF16)
            output_part_ref[...] += dot_lanes(mixture, pair_grad)
        return carry

    lax.fori_loop(0, rows // together, some_rows, 0)


def pair_sums(features, pair, labels, weights, residues):
    row_count, width, pair_width = pair.shape
    channels = features[0].shape[1]
    block = math.gcd(8, row_count)
    together = math.gcd(2, block)
    bins = weights[4].shape[1]
    whole = lambda array: pl.BlockSpec(array.shape, lambda r: (0,) * array.ndim)
    blocked = lambda array: pl.BlockSpec(
        (block,) + array.shape[1:], lambda r: (r,) + (0,) * (array.ndim - 1)
    )
    shapes = [
        (1, width),
        (bins, pair_width + TILE),
        (HEADS * HEAD_DIM, pair_width),
    ]
    pairs = row_count * width
    return pl.pallas_call(
        functools.partial(pair_kernel, together, residues),
        grid=(row_count // block,),
        in_specs=[blocked(one) for one in features]
        + [blocked(pair), blocked(labels)]
        + [whole(one) for one in weights],
        out_specs=[pl.BlockSpec(shape, lambda r: (0, 0)) for shape in shapes],
        out_shape=[jax.ShapeDtypeStruct(shape, F32) for shape in shapes],
        compiler_params=pltpu.CompilerParams(vmem_limit_bytes=48 * 2**20),
        cost_estimate=pl.CostEstimate(
            flops=pairs * 2 * 256 * 1152,
            bytes_accessed=pairs * (len(features) * channels + pair_width) * 2,
            transcendentals=0,
        ),
        name="pair_sums",
    )(*features, pair, labels, *weights)


def partners(count, step):
    if count & (count - 1) == 0:
        return [(one, one ^ step) for one in range(count)]
    return [(one, (one + step) % count) for one in range(count)]


def towards(me, count, step):
    if count & (count - 1) == 0:
        return me ^ step
    return lax.rem(me + step, count)


def origin(me, count, step):
    if count & (count - 1) == 0:
        return me ^ step
    return lax.rem(me - step + count, count)


def on_device(
    tmpl_act,
    tmpl_bins,
    tmpl_mask,
    tmpl_aatype,
    pair_act,
    labels,
    bin_embed,
    row_embed,
    col_embed,
    mask_embed,
    layer_gain,
    w_in,
    w_out,
    final_gain,
    w_query,
    w_keyval,
    w_output,
    head_weight,
    head_bias,
):
    group_count = lax.axis_size("tmpl")
    col_count = lax.axis_size("col")
    residues = tmpl_mask.shape[1]
    group_rows = tmpl_bins.shape[2]
    col_width = tmpl_bins.shape[3]
    row_count = group_rows // col_count
    channels = tmpl_act.shape[3]
    pair_width = pair_act.shape[2]
    tmpl_me = lax.axis_index("tmpl")
    col_me = lax.axis_index("col")
    row_offset = lax.axis_index("row") * group_rows
    levels = bin_embed.shape[0]
    kinds = row_embed.shape[0]

    def pair_block(array, block):
        return lax.dynamic_slice_in_dim(array, block * col_width, col_width, axis=1)

    pair_parts, label_parts = [], []
    for step in range(col_count):
        block = towards(col_me, col_count, step)
        pair, label = pair_block(pair_act, block), pair_block(labels, block)
        if step:
            pair = lax.ppermute(pair, "col", partners(col_count, step))
            label = lax.ppermute(label, "col", partners(col_count, step))
        pair_parts.append(pair)
        label_parts.append(label)

    masks, types = tmpl_mask[0], tmpl_aatype[0]
    col_offset = col_me * col_width
    colmask = lax.dynamic_slice_in_dim(masks, col_offset, col_width)[None, :]
    col_types = lax.dynamic_slice_in_dim(types, col_offset, col_width)
    kind_iota = jnp.arange(padded(kinds), dtype=jnp.int32)
    colhot = (col_types[None, :] == kind_iota[:, None]).astype(BF16)
    high = lax.reduce_precision(mask_embed, 8, 7)
    middle = lax.reduce_precision(mask_embed - high, 8, 7)
    low = mask_embed - high - middle
    mask_terms = jnp.stack([high, middle, low], axis=1).astype(BF16)
    embed = jnp.concatenate(
        [
            jnp.eye(channels, dtype=BF16),
            pad_columns(jnp.concatenate([bin_embed.T, mask_terms], axis=1)),
            pad_columns(col_embed.T),
            pad_columns(row_embed.T),
        ],
        axis=1,
    )
    gains = jnp.concatenate([layer_gain, final_gain[None]], axis=0)[:, :, None]
    w_in_t = jnp.swapaxes(w_in, 1, 2)
    w_out_t = jnp.swapaxes(w_out, 1, 2)
    weights = (
        jnp.concatenate([w_query.T, jnp.eye(pair_width, dtype=BF16)], axis=0),
        w_keyval.T,
        w_output.T,
        head_weight.T,
        head_weight,
        head_bias[:, None],
    )

    order = [group_count - 1] + list(range(1, group_count - 1)) + [0]
    sums = []
    for step in range(col_count):
        block = origin(col_me, col_count, step)
        features = []
        for turn in order:
            group = towards(tmpl_me, group_count, turn)
            offset = group * (residues // group_count) + row_offset + block * row_count
            place = jnp.stack([group, block, offset]).astype(jnp.int32)
            part = template_features(
                tmpl_act[0],
                tmpl_bins[0],
                place,
                masks,
                types,
                colmask,
                colhot,
                embed,
                gains,
                w_in_t,
                w_out_t,
                levels,
                row_count,
            )
            if turn:
                part = lax.ppermute(part, "tmpl", partners(group_count, turn))
            features.append(part)
        sums.append(pair_sums(features, pair_parts[step], label_parts[step], weights, residues))

    loss_part, head_part, output_part = [sum(parts[1:], parts[0]) for parts in zip(*sums)]
    bins = head_weight.shape[1]
    joined = jnp.concatenate(
        [head_part.reshape(-1), output_part.reshape(-1), jnp.sum(loss_part)[None]]
    )
    joined = lax.psum(joined, ("tmpl", "row", "col"))
    head_size = head_part.size
    head_all = joined[:head_size].reshape(head_part.shape)
    head_sum = head_all[:, :pair_width].T
    bias_sum = head_all[:, pair_width]
    output_sum = joined[head_size:-1].reshape(output_part.shape)
    loss_sum = joined[-1]
    squares = (
        jnp.sum(head_sum * head_sum)
        + jnp.sum(bias_sum * bias_sum)
        + jnp.sum(output_sum * output_sum)
    )
    factor = CLIP_NORM / jnp.maximum(jnp.sqrt(squares), CLIP_NORM)
    return (
        loss_sum / float(residues * residues),
        head_sum * factor,
        bias_sum * factor,
        output_sum * factor,
    )


def solution(mesh):
    in_specs = (
        P("tmpl", None, "row", None, "col"),
        P("tmpl", None, "row", "col"),
        P("tmpl", None),
        P("tmpl", None),
        P(("tmpl", "row", "col"), None, None),
        P(("tmpl", "row", "col"), None),
        P(),
        P(),
        P(),
        P(),
        P(),
        P(),
        P(),
        P(),
        P(),
        P(),
        P(),
        P(),
        P(),
    )
    out_specs = (P(), P(), P(), P())
    return jax.shard_map(
        on_device, mesh=mesh, in_specs=in_specs, out_specs=out_specs, check_vma=False
    )
```
